512 devices in a mesh: pix: 128 (over z, x_lo, y), comp: 4 (over x_hi, core).
Axes of the slice: x: 4 (x_hi: 2, x_lo: 2; x = x_hi * 2 + x_lo), y: 4, z: 16, core: 2. Of those that a mesh axis runs over, the one named last changes fastest.
Arguments:
- atmos_state: bfloat16 [2, 8, 4096, 128], P(None, None, 'pix'), may hold values from -6 to 6
- ocean_state: bfloat16 [2, 8, 4096, 128], P(None, None, 'pix'), may hold values from -6 to 6
- conv_weight: bfloat16 [4, 2, 9, 128, 128], P('comp'), may hold values from -0.1875 to 0.1875
- rotation: int32 [128, 2], P('pix'), may hold values from 0 to 3
- sea_mask: int32 [8, 4096], P(None, 'pix'), may hold values 0 or 1
Outputs:
- atmos_next: bfloat16 [2, 8, 4096, 128], P(None, 'comp', 'pix')
- ocean_next: bfloat16 [2, 8, 4096, 128], P(None, 'comp', 'pix')
The draws below stay inside these ranges and needn't reach their ends.
All inputs are finite; a program needn't handle non-finite values. No bound on the sum of `sea_mask` on one device may be relied on, other than what follows from the above.
Results may differ from the reference program's by a relative error of at most 0.025.
Values may be sent and summed in bfloat16 or wider, within the bound.
No kernel may reach another device: no remote copies, remote signals or barrier semaphores. Data moves between devices by JAX's collectives and lax.ppermute only.
A program may use at most 64 MiB of HBM per device.

```python
import jax
import jax.numpy as jnp

C = 128
M = 2
R = 8
SEGMENTS = 4
STEPS = 2
TILES = 128
NCOL = 4096


def plant(result, own_key, smallest, top_value):
    shape = result.shape
    spot = [jax.random.randint(jax.random.fold_in(own_key, axis), (), 0, shape[axis]) for axis in range(len(shape))]
    result = result.at[tuple(spot)].set(smallest)
    longest = shape.index(max(shape))
    spot[longest] = (spot[longest] + 1) % shape[longest]
    return result.at[tuple(spot)].set(top_value)


def levels(key, dims, pieces, smallest, largest):
    factor_of = 1.0
    for dim, parts in pieces:
        draws = jax.random.uniform(jax.random.fold_in(jax.random.fold_in(key, 6), dim), (parts,), jnp.float32, smallest / len(pieces), largest / len(pieces))
        factor_of = factor_of * jnp.repeat(jnp.exp(draws), dims[dim] // parts).reshape((-1,) + (1,) * (len(dims) - 1 - dim))
    return factor_of


def scatter_about(stream_key, shape, width, most, shards=(), dtype=jnp.bfloat16):
    result = jax.random.normal(stream_key, shape, jnp.float32) * width
    if len(shards) > 0:
        result = levels(stream_key, shape, shards, -0.22, 0.18) * result
    return jnp.clip(result, min=-most, max=most).astype(dtype)


def setup_inputs(seed: int = 0) -> dict:
    splits = jax.random.split(jax.random.key(seed), 6)
    atmos_state = scatter_about(splits[0], (M, R, NCOL, C), 1.0, 6.0, ((2, 128),))
    ocean_state = scatter_about(splits[1], (M, R, NCOL, C), 1.0, 6.0, ((2, 128),))
    conv_weight = scatter_about(splits[2], (SEGMENTS, 2, 9, C, C), (9 * C) ** -0.5, 0.1875, ((0, 4),))
    rotation = plant(jax.random.randint(splits[3], (TILES, 2), 0, 4), jax.random.fold_in(splits[3], 1), 0, 3).astype(jnp.int32)
    sea_mask = plant((jax.random.randint(splits[4], (R, NCOL), 0, 10) < 7).astype(jnp.int32), jax.random.fold_in(splits[4], 1), 0, 1)
    return dict(atmos_state=atmos_state, ocean_state=ocean_state, conv_weight=conv_weight, rotation=rotation, sea_mask=sea_mask)


def turn_pairs(column, turn_code):
    half_width = column.shape[-1] // 2
    first_part = column[..., :half_width].astype(jnp.float32)
    second_part = column[..., half_width:].astype(jnp.float32)
    cosine = jnp.where(turn_code == 0, 1.0, jnp.where(turn_code == 2, -1.0, 0.0)).astype(jnp.float32)[..., None]
    sine_term = jnp.where(turn_code == 1, 1.0, jnp.where(turn_code == 3, -1.0, 0.0)).astype(jnp.float32)[..., None]
    turned = jnp.concatenate([cosine * first_part - sine_term * second_part, sine_term * first_part + cosine * second_part], axis=-1)
    return turned.astype(jnp.bfloat16)


def convolve(field_in, weights, rotation):
    tile_count = rotation.shape[0]
    row_count, columns, channels = field_in.shape
    tile_width = columns // tile_count
    blocks = field_in.reshape(row_count, tile_count, tile_width, channels)
    left_column = turn_pairs(jnp.roll(blocks[:, :, tile_width - 1], 1, axis=1), rotation[:, 0][None, :])
    right_column = turn_pairs(jnp.roll(blocks[:, :, 0], -1, axis=1), rotation[:, 1][None, :])
    padded = jnp.concatenate([left_column[:, :, None], blocks, right_column[:, :, None]], axis=2)
    padded = jnp.pad(padded, ((1, 1), (0, 0), (0, 0), (0, 0)))
    total_sum = jnp.zeros((row_count * tile_count * tile_width, channels), jnp.float32)
    for offset in range(9):
        row_shift, column_shift = offset // 3, offset % 3
        window = padded[row_shift:row_shift + row_count, :, column_shift:column_shift + tile_width].reshape(-1, channels)
        total_sum = total_sum + jnp.dot(window, weights[offset], preferred_element_type=jnp.float32)
    return total_sum.reshape(row_count, columns, channels)


def residual_block(field_in, weights, rotation, base_field, gate_field):
    inner_field = jax.nn.gelu(convolve(field_in, weights[0], rotation)).astype(jnp.bfloat16)
    return (base_field.astype(jnp.float32) + gate_field * convolve(inner_field, weights[1], rotation)).astype(jnp.bfloat16)


def reference(atmos_state, ocean_state, conv_weight, rotation, sea_mask):
    sea_field = sea_mask.astype(jnp.float32)[:, :, None]
    atmos_list = []
    ocean_list = []
    for member_index in range(M):
        atmos_now = atmos_state[member_index]
        ocean_now = ocean_state[member_index]
        for step_index in range(STEPS):
            hidden = (atmos_now.astype(jnp.float32) + sea_field * ocean_now.astype(jnp.float32)).astype(jnp.bfloat16)
            for section in range(SEGMENTS - 1):
                hidden = residual_block(hidden, conv_weight[section], rotation, hidden, jnp.float32(1.0))
            flux_in = (hidden.astype(jnp.float32) + ocean_now.astype(jnp.float32)).astype(jnp.bfloat16)
            ocean_now = residual_block(flux_in, conv_weight[SEGMENTS - 1], rotation, ocean_now, sea_field)
            atmos_now = hidden
        atmos_list.append(atmos_now)
        ocean_list.append(ocean_now)
    return jnp.stack(atmos_list), jnp.stack(ocean_list)
```

```python
import functools

import jax
import jax.numpy as jnp
from jax import lax
from jax.experimental import pallas as pl
from jax.experimental.pallas import tpu as pltpu
from jax.sharding import PartitionSpec as P

STEPS = 2
BF = jnp.bfloat16
F32 = jnp.float32

DEPTH = 16
WIDTH = 32
OWN = DEPTH + 2
RIGHT = OWN + WIDTH + 2
TOTAL = RIGHT + DEPTH


def pack_kernel(atmos_ref, ocean_ref, rotation_ref, mask_ref, fields_ref, up_ref, down_ref, tile):
    for index, ref in enumerate((atmos_ref, ocean_ref)):
        value = ref[...].astype(F32).reshape(16, WIDTH, 128)
        value = jnp.swapaxes(value, 0, 1).astype(BF)
        fields_ref[pl.ds(index * WIDTH, WIDTH)] = value
        up_ref[pl.ds(index * DEPTH, DEPTH)] = value[WIDTH - DEPTH :]
        down_ref[pl.ds(index * DEPTH, DEPTH)] = value[:DEPTH]
    lane = lax.broadcasted_iota(jnp.int32, (16, 128), 1)
    first = rotation_ref[0, 0].astype(F32)
    second = rotation_ref[0, 1].astype(F32)
    tile[...] = jnp.where(lane == 64, first, jnp.where(lane == 65, second, 0.0))
    mask = mask_ref[...].astype(F32)
    tile[0:8, 0:WIDTH] = mask
    tile[8:16, 0:WIDTH] = mask
    packed = tile[...].astype(BF)
    fields_ref[2 * WIDTH] = packed
    up_ref[2 * DEPTH] = packed
    down_ref[2 * DEPTH] = packed


def conv(source, weight, done):
    start = done + 1
    count = TOTAL - 2 * start
    left = jnp.concatenate(
        [source[pl.ds(start - 1, count)], source[pl.ds(start, count)], source[pl.ds(start + 1, count)]], axis=-1
    ).reshape(count * 16, 384)
    right = jnp.concatenate(
        [jnp.concatenate([weight[3 * a + b] for a in range(3)], axis=1) for b in range(3)], axis=0
    )
    product = lax.dot_general(left, right, (((1,), (0,)), ((), ())), preferred_element_type=F32)
    above, here, below = (product[:, 128 * a : 128 * a + 128].reshape(count * 2, 8, 128) for a in range(3))
    row = lax.broadcasted_iota(jnp.int32, (1, 8, 128), 1)
    above = jnp.where(row == 0, 0.0, pltpu.roll(above, 1, 1))
    below = jnp.where(row == 7, 0.0, pltpu.roll(below, 7, 1))
    return (here + above + below).reshape(count, 16, 128)


def turn_factors(code):
    lane = lax.broadcasted_iota(jnp.int32, (16, 128), 1)
    side = jnp.where(lane < 64, -1.0, 1.0)
    keep = jnp.where(code == 0.0, 1.0, jnp.where(code == 2.0, -1.0, 0.0))
    swap = jnp.where(code == 1.0, side, jnp.where(code == 3.0, -side, 0.0))
    return keep, swap


def main_kernel(
    fields_ref, before_ref, after_ref, own_ref, sibling_ref, far_ref, far_sibling_ref, atmos_out, ocean_out,
    weight, hidden, inner, ocean, sea, flux, final, semaphores,
):
    comp = lax.axis_index("comp")
    core = lax.rem(comp, 2)
    half = lax.div(comp, 2)
    places = (comp, half * 2 + 1 - core, (1 - half) * 2 + core, (1 - half) * 2 + 1 - core)
    copies = [
        pltpu.make_async_copy(ref.at[0], weight.at[place], semaphores.at[index])
        for index, (ref, place) in enumerate(zip((own_ref, sibling_ref, far_ref, far_sibling_ref), places))
    ]
    for copy in copies:
        copy.start()

    def broadcast(tile, column):
        return jnp.broadcast_to(tile[:, column : column + 1], (16, 128))

    own_tile = fields_ref[2 * WIDTH].astype(F32)
    before_tile = before_ref[2 * DEPTH].astype(F32)
    after_tile = after_ref[2 * DEPTH].astype(F32)
    seams = (
        (DEPTH, OWN, turn_factors(broadcast(before_tile, 65))),
        (DEPTH + 1, DEPTH - 1, turn_factors(broadcast(own_tile, 64))),
        (OWN + WIDTH, RIGHT, turn_factors(broadcast(own_tile, 65))),
        (RIGHT - 1, OWN + WIDTH - 1, turn_factors(broadcast(after_tile, 64))),
    )

    def close_seams(ref):
        for place, origin, (keep, swap) in seams:
            value = ref[origin].astype(F32)
            ref[place] = (keep * value + swap * pltpu.roll(value, 64, 1)).astype(BF)

    for ref, offset in ((hidden, 0), (ocean, 1)):
        ref[pl.ds(0, DEPTH)] = before_ref[pl.ds(offset * DEPTH, DEPTH)]
        ref[pl.ds(OWN, WIDTH)] = fields_ref[pl.ds(offset * WIDTH, WIDTH)]
        ref[pl.ds(RIGHT, DEPTH)] = after_ref[pl.ds(offset * DEPTH, DEPTH)]
    nothing = jnp.zeros((2, 16, 128), BF)
    for ref in (hidden, ocean, sea):
        ref[pl.ds(DEPTH, 2)] = nothing
        ref[pl.ds(RIGHT - 2, 2)] = nothing
    for column in range(DEPTH):
        sea[column] = broadcast(before_tile, WIDTH - DEPTH + column).astype(BF)
        sea[RIGHT + column] = broadcast(after_tile, column).astype(BF)
    for column in range(WIDTH):
        sea[OWN + column] = broadcast(own_tile, column).astype(BF)
    for copy in copies:
        copy.wait()

    done = 0
    for step in range(STEPS):
        span = pl.ds(done, TOTAL - 2 * done)
        hidden[span] = (hidden[span].astype(F32) + sea[span].astype(F32) * ocean[span].astype(F32)).astype(BF)
        close_seams(hidden)
        for section in range(4):
            if section == 3:
                span = pl.ds(done, TOTAL - 2 * done)
                flux[span] = (hidden[span].astype(F32) + ocean[span].astype(F32)).astype(BF)
                close_seams(flux)
            source = flux if section == 3 else hidden
            value = jax.nn.gelu(conv(source, weight.at[section, 0], done)).astype(BF)
            done += 1
            inner[pl.ds(done, TOTAL - 2 * done)] = value
            close_seams(inner)
            value = conv(inner, weight.at[section, 1], done)
            done += 1
            span = pl.ds(done, TOTAL - 2 * done)
            if section == 3:
                ocean[span] = (ocean[span].astype(F32) + sea[span].astype(F32) * value).astype(BF)
            else:
                hidden[span] = (hidden[span].astype(F32) + value).astype(BF)
                close_seams(hidden)

    for source, out in ((hidden, atmos_out), (ocean, ocean_out)):
        final[...] = jnp.swapaxes(source[pl.ds(OWN, WIDTH)].astype(F32), 0, 1)
        for member in range(2):
            out[member] = final[pl.ds(member * 8 + 2 * comp, 2)].astype(BF)


def per_device(atmos_state, ocean_state, conv_weight, rotation, sea_mask):
    tiles = lax.axis_size("pix")
    vmem = pl.BlockSpec(memory_space=pltpu.VMEM)
    fields, up, down = pl.pallas_call(
        pack_kernel,
        out_shape=(
            jax.ShapeDtypeStruct((2 * WIDTH + 1, 16, 128), BF),
            jax.ShapeDtypeStruct((2 * DEPTH + 1, 16, 128), BF),
            jax.ShapeDtypeStruct((2 * DEPTH + 1, 16, 128), BF),
        ),
        in_specs=[vmem, vmem, pl.BlockSpec(memory_space=pltpu.SMEM), vmem],
        out_specs=(vmem, vmem, vmem),
        scratch_shapes=[pltpu.VMEM((16, 128), F32)],
    )(atmos_state, ocean_state, rotation, sea_mask)

    names = ("pix", "comp")
    flip = 4 if tiles % 8 == 0 else 0
    swap = [(p * 4 + c, p * 4 + (c ^ 1)) for p in range(tiles) for c in range(4)]
    across = [(p * 4 + c, (p ^ flip) * 4 + (c ^ 2)) for p in range(tiles) for c in range(4)]
    far = lax.ppermute(conv_weight, names, across)
    sibling = lax.ppermute(conv_weight, names, swap)
    rightward = [(i, (i + 1) % tiles) for i in range(tiles)]
    before = lax.ppermute(up, "pix", rightward)
    after = lax.ppermute(down, "pix", [(j, i) for i, j in rightward])
    far_sibling = lax.ppermute(far, names, swap)

    anywhere = pl.BlockSpec(memory_space=pl.ANY)
    band = jax.ShapeDtypeStruct((2, 2, WIDTH, 128), BF)
    field = pltpu.VMEM((TOTAL, 16, 128), BF)
    return pl.pallas_call(
        main_kernel,
        out_shape=(band, band),
        in_specs=[vmem, vmem, vmem] + [anywhere] * 4,
        out_specs=(vmem, vmem),
        scratch_shapes=[
            pltpu.VMEM((4,) + conv_weight.shape[1:], BF),
            field,
            field,
            field,
            field,
            field,
            pltpu.VMEM((16, WIDTH, 128), F32),
            pltpu.SemaphoreType.DMA((4,)),
        ],
        compiler_params=pltpu.CompilerParams(vmem_limit_bytes=40 << 20),
    )(fields, before, after, conv_weight, sibling, far, far_sibling)


def solution(mesh):
    in_specs = (
        P(None, None, "pix", None),
        P(None, None, "pix", None),
        P("comp", None, None, None, None),
        P("pix", None),
        P(None, "pix"),
    )
    out_specs = (P(None, "comp", "pix", None), P(None, "comp", "pix", None))
    return jax.shard_map(
        per_device, mesh=mesh, in_specs=in_specs, out_specs=out_specs, check_vma=False
    )
```

```python
import functools

import jax
import jax.numpy as jnp
from jax import lax
from jax.experimental import pallas as pl
from jax.experimental.pallas import tpu as pltpu
from jax.sharding import PartitionSpec as P

STEPS = 2
BF = jnp.bfloat16
F32 = jnp.float32

DEPTH = 16
WIDTH = 32
OWN = DEPTH + 2
RIGHT = OWN + WIDTH + 2
TOTAL = RIGHT + DEPTH
CUT = 48


def pack_kernel(atmos_ref, ocean_ref, rotation_ref, mask_ref, fields_ref, up_ref, down_ref, tile):
    for index, ref in enumerate((atmos_ref, ocean_ref)):
        value = ref[...].astype(F32).reshape(16, WIDTH, 128)
        value = jnp.swapaxes(value, 0, 1).astype(BF)
        fields_ref[pl.ds(index * WIDTH, WIDTH)] = value
        up_ref[pl.ds(index * DEPTH, DEPTH)] = value[WIDTH - DEPTH :]
        down_ref[pl.ds(index * DEPTH, DEPTH)] = value[:DEPTH]
    lane = lax.broadcasted_iota(jnp.int32, (16, 128), 1)
    first = rotation_ref[0, 0].astype(F32)
    second = rotation_ref[0, 1].astype(F32)
    tile[...] = jnp.where(lane == 64, first, jnp.where(lane == 65, second, 0.0))
    mask = mask_ref[...].astype(F32)
    tile[0:8, 0:WIDTH] = mask
    tile[8:16, 0:WIDTH] = mask
    packed = tile[...].astype(BF)
    fields_ref[2 * WIDTH] = packed
    up_ref[2 * DEPTH] = packed
    down_ref[2 * DEPTH] = packed


def product(source, weight, start, stop):
    count = stop - start
    left = jnp.concatenate([source[pl.ds(start + b - 1, count)] for b in range(3)], axis=-1)
    right = jnp.concatenate(
        [jnp.concatenate([weight[3 * a + b] for a in range(3)], axis=1) for b in range(3)], axis=0
    )
    return lax.dot_general(
        left.reshape(count * 16, 384), right, (((1,), (0,)), ((), ())), preferred_element_type=F32
    )


def add_rows(value, count):
    above, here, below = (value[:, 128 * a : 128 * a + 128].reshape(count * 2, 8, 128) for a in range(3))
    row = lax.broadcasted_iota(jnp.int32, (1, 8, 128), 1)
    above = jnp.where(row == 0, 0.0, pltpu.roll(above, 1, 1))
    below = jnp.where(row == 7, 0.0, pltpu.roll(below, 7, 1))
    return (here + above + below).reshape(count, 16, 128)


def gelu(value):
    half = 0.5 * value
    return half + half * jnp.tanh(value * (0.7978845608028654 + 0.035677408136300125 * (value * value)))


SEAMS = ((DEPTH, OWN), (DEPTH + 1, DEPTH - 1), (OWN + WIDTH, RIGHT), (RIGHT - 1, OWN + WIDTH - 1))


def close_seams(ref, factors, which):
    for index in which:
        place, origin = SEAMS[index]
        value = ref[origin].astype(F32)
        turned = factors[2 * index].astype(F32) * value + factors[2 * index + 1].astype(F32) * pltpu.roll(value, 64, 1)
        ref[place] = turned.astype(BF)


def turn_factors(code):
    lane = lax.broadcasted_iota(jnp.int32, (16, 128), 1)
    side = jnp.where(lane < 64, -1.0, 1.0)
    keep = jnp.where(code == 0.0, 1.0, jnp.where(code == 2.0, -1.0, 0.0))
    swap = jnp.where(code == 1.0, side, jnp.where(code == 3.0, -side, 0.0))
    return keep.astype(BF), swap.astype(BF)


def state_kernel(fields_ref, before_ref, after_ref, own_ref, sibling_ref, state_ref, weight_ref, semaphores):
    comp = lax.axis_index("comp")
    copies = (
        pltpu.make_async_copy(own_ref.at[0], weight_ref.at[comp], semaphores.at[0]),
        pltpu.make_async_copy(sibling_ref.at[0], weight_ref.at[comp + 1 - 2 * lax.rem(comp, 2)], semaphores.at[1]),
    )
    for copy in copies:
        copy.start()

    def broadcast(tile, column):
        return jnp.broadcast_to(tile[:, column : column + 1], (16, 128))

    own_tile = fields_ref[2 * WIDTH].astype(F32)
    before_tile = before_ref[2 * DEPTH].astype(F32)
    after_tile = after_ref[2 * DEPTH].astype(F32)
    hidden, ocean, sea, factors = (
        state_ref.at[pl.ds(TOTAL * index, TOTAL if index < 3 else 2 * len(SEAMS))] for index in range(4)
    )
    for index, (tile, lane) in enumerate(((before_tile, 65), (own_tile, 64), (own_tile, 65), (after_tile, 64))):
        factors[2 * index], factors[2 * index + 1] = turn_factors(broadcast(tile, lane))
    for column in range(DEPTH):
        sea[column] = broadcast(before_tile, WIDTH - DEPTH + column).astype(BF)
        sea[RIGHT + column] = broadcast(after_tile, column).astype(BF)
    for column in range(WIDTH):
        sea[OWN + column] = broadcast(own_tile, column).astype(BF)
    nothing = jnp.zeros((2, 16, 128), BF)
    for ref in (ocean, sea):
        ref[pl.ds(DEPTH, 2)] = nothing
        ref[pl.ds(RIGHT - 2, 2)] = nothing
    for ref, origin, count, place in (
        (before_ref, 0, DEPTH, 0),
        (fields_ref, 0, WIDTH, OWN),
        (after_ref, 0, DEPTH, RIGHT),
    ):
        span = pl.ds(place, count)
        ocean_value = ref[pl.ds(origin + count, count)]
        ocean[span] = ocean_value
        atmos_value = ref[pl.ds(origin, count)].astype(F32)
        hidden[span] = (atmos_value + sea[span].astype(F32) * ocean_value.astype(F32)).astype(BF)
    close_seams(hidden, factors, range(4))
    for copy in copies:
        copy.wait()


def main_kernel(
    state_ref, weight_ref, far_ref, far_sibling_ref, atmos_out, ocean_out, weight_out,
    hidden_ref, inner, ocean_ref, flux, final, semaphores,
):
    comp = lax.axis_index("comp")
    core = lax.rem(comp, 2)
    other = 2 - 2 * lax.div(comp, 2)
    copies = (
        pltpu.make_async_copy(far_ref.at[0], weight_out.at[other + core], semaphores.at[0]),
        pltpu.make_async_copy(far_sibling_ref.at[0], weight_out.at[other + 1 - core], semaphores.at[1]),
    )
    for copy in copies:
        copy.start()
    hidden, ocean, sea, factors = (
        state_ref.at[pl.ds(TOTAL * index, TOTAL if index < 3 else 2 * len(SEAMS))] for index in range(4)
    )
    for copy in copies:
        copy.wait()

    def load(ref, span):
        return ref[span].astype(F32)

    def convolve(source, weight, done, finish, out):
        bounds = (done, CUT - done, TOTAL - done)
        for part in range(2):
            start, stop = bounds[part : part + 2]
            span = pl.ds(start, stop - start)
            value = add_rows(product(source, weight, start, stop), stop - start)
            out[span] = finish(span, value).astype(BF)
            if done < DEPTH:
                close_seams(out, factors, (0, 1) if part == 0 else (2, 3))

    done = 0
    for step in range(STEPS):
        if step > 0:
            for start, stop, seams in ((done, CUT - done, (0, 1)), (CUT - done, TOTAL - done, (2, 3))):
                span = pl.ds(start, stop - start)
                hidden_ref[span] = (load(hidden, span) + load(sea, span) * load(ocean, span)).astype(BF)
                close_seams(hidden_ref, factors, seams)
        for section in range(4):
            source = hidden
            if section == 3:
                source = flux
                for start, stop, seams in ((done, CUT - done, (0, 1)), (CUT - done, TOTAL - done, (2, 3))):
                    span = pl.ds(start, stop - start)
                    flux[span] = (load(hidden, span) + load(ocean, span)).astype(BF)
                    close_seams(flux, factors, seams)
            weight = weight_out.at[section]
            done += 1
            convolve(source, weight.at[0], done, lambda span, value: gelu(value), inner)
            done += 1
            if section == 3:
                base = ocean
                convolve(
                    inner, weight.at[1], done,
                    lambda span, value: load(base, span) + load(sea, span) * value, ocean_ref,
                )
                ocean = ocean_ref
            else:
                base = hidden
                convolve(inner, weight.at[1], done, lambda span, value: load(base, span) + value, hidden_ref)
                hidden = hidden_ref

    for source, out in ((hidden, atmos_out), (ocean, ocean_out)):
        final[...] = jnp.swapaxes(source[pl.ds(OWN, WIDTH)].astype(F32), 0, 1)
        for member in range(2):
            out[member] = final[pl.ds(member * 8 + 2 * comp, 2)].astype(BF)


def per_device(atmos_state, ocean_state, conv_weight, rotation, sea_mask):
    tiles = lax.axis_size("pix")
    vmem = pl.BlockSpec(memory_space=pltpu.VMEM)
    fields, up, down = pl.pallas_call(
        pack_kernel,
        out_shape=(
            jax.ShapeDtypeStruct((2 * WIDTH + 1, 16, 128), BF),
            jax.ShapeDtypeStruct((2 * DEPTH + 1, 16, 128), BF),
            jax.ShapeDtypeStruct((2 * DEPTH + 1, 16, 128), BF),
        ),
        in_specs=[vmem, vmem, pl.BlockSpec(memory_space=pltpu.SMEM), vmem],
        out_specs=(vmem, vmem, vmem),
        scratch_shapes=[pltpu.VMEM((16, 128), F32)],
    )(atmos_state, ocean_state, rotation, sea_mask)

    names = ("pix", "comp")
    flip = 4 if tiles % 8 == 0 else 0
    swap = [(p * 4 + c, p * 4 + (c ^ 1)) for p in range(tiles) for c in range(4)]
    across = [(p * 4 + c, (p ^ flip) * 4 + (c ^ 2)) for p in range(tiles) for c in range(4)]
    far = lax.ppermute(conv_weight, names, across)
    sibling = lax.ppermute(conv_weight, names, swap)
    rightward = [(i, (i + 1) % tiles) for i in range(tiles)]
    before = lax.ppermute(up, "pix", rightward)
    after = lax.ppermute(down, "pix", [(j, i) for i, j in rightward])
    far, before, after = lax.optimization_barrier((far, before, after))
    far_sibling = lax.ppermute(far, names, swap)

    anywhere = pl.BlockSpec(memory_space=pl.ANY)
    all_weights = jax.ShapeDtypeStruct((4,) + conv_weight.shape[1:], BF)
    params = pltpu.CompilerParams(vmem_limit_bytes=40 << 20)
    state, weight = pl.pallas_call(
        state_kernel,
        out_shape=(jax.ShapeDtypeStruct((3 * TOTAL + 2 * len(SEAMS), 16, 128), BF), all_weights),
        in_specs=[vmem, vmem, vmem, anywhere, anywhere],
        out_specs=(vmem, vmem),
        scratch_shapes=[pltpu.SemaphoreType.DMA((2,))],
        compiler_params=params,
    )(fields, before, after, conv_weight, sibling)

    band = jax.ShapeDtypeStruct((2, 2, WIDTH, 128), BF)
    field = pltpu.VMEM((TOTAL, 16, 128), BF)
    return pl.pallas_call(
        main_kernel,
        out_shape=(band, band, all_weights),
        in_specs=[vmem, vmem, anywhere, anywhere],
        out_specs=(vmem, vmem, vmem),
        input_output_aliases={1: 2},
        scratch_shapes=[
            field,
            field,
            field,
            field,
            pltpu.VMEM((16, WIDTH, 128), F32),
            pltpu.SemaphoreType.DMA((2,)),
        ],
        compiler_params=params,
    )(state, weight, far, far_sibling)[:2]


def solution(mesh):
    in_specs = (
        P(None, None, "pix", None),
        P(None, None, "pix", None),
        P("comp", None, None, None, None),
        P("pix", None),
        P(None, "pix"),
    )
    out_specs = (P(None, "comp", "pix", None), P(None, "comp", "pix", None))
    return jax.shard_map(
        per_device, mesh=mesh, in_specs=in_specs, out_specs=out_specs, check_vma=False
    )
```

```python
import functools

import jax
import jax.numpy as jnp
from jax import lax
from jax.experimental import pallas as pl
from jax.experimental.pallas import tpu as pltpu
from jax.sharding import PartitionSpec as P

STEPS = 2
BF = jnp.bfloat16
F32 = jnp.float32

DEPTH = 16
WIDTH = 32
OWN = DEPTH + 2
RIGHT = OWN + WIDTH + 2
TOTAL = RIGHT + DEPTH
CUT = 48


def pack_kernel(atmos_ref, ocean_ref, rotation_ref, mask_ref, fields_ref, down_ref, up_ref, tile):
    for index, ref in enumerate((atmos_ref, ocean_ref)):
        value = ref[...].astype(F32).reshape(16, WIDTH, 128)
        value = jnp.swapaxes(value, 0, 1).astype(BF)
        fields_ref[pl.ds(index * WIDTH, WIDTH)] = value
        up_ref[pl.ds(index * DEPTH, DEPTH)] = value[WIDTH - DEPTH :]
        down_ref[pl.ds(index * DEPTH, DEPTH)] = value[:DEPTH]
    lane = lax.broadcasted_iota(jnp.int32, (16, 128), 1)
    first = rotation_ref[0, 0].astype(F32)
    second = rotation_ref[0, 1].astype(F32)
    tile[...] = jnp.where(lane == 64, first, jnp.where(lane == 65, second, 0.0))
    mask = mask_ref[...].astype(F32)
    tile[0:8, 0:WIDTH] = mask
    tile[8:16, 0:WIDTH] = mask
    packed = tile[...].astype(BF)
    fields_ref[2 * WIDTH] = packed
    up_ref[2 * DEPTH] = packed
    down_ref[2 * DEPTH] = packed


def product(source, weight, start, stop):
    count = stop - start
    left = jnp.concatenate([source[pl.ds(start + b - 1, count)] for b in range(3)], axis=-1)
    right = jnp.concatenate([jnp.concatenate([weight(3 * a + b) for a in range(3)], axis=1) for b in range(3)], axis=0)
    return lax.dot_general(
        left.reshape(count * 16, 384), right, (((1,), (0,)), ((), ())), preferred_element_type=F32
    )


def add_rows(value, count):
    above, here, below = (value[:, 128 * a : 128 * a + 128].reshape(count * 2, 8, 128) for a in range(3))
    row = lax.broadcasted_iota(jnp.int32, (1, 8, 128), 1)
    above = jnp.where(row == 0, 0.0, pltpu.roll(above, 1, 1))
    below = jnp.where(row == 7, 0.0, pltpu.roll(below, 7, 1))
    return (here + above + below).reshape(count, 16, 128)


def gelu(value):
    half = 0.5 * value
    return half + half * jnp.tanh(value * (0.7978845608028654 + 0.035677408136300125 * (value * value)))


SEAMS = ((DEPTH, OWN), (DEPTH + 1, DEPTH - 1), (OWN + WIDTH, RIGHT), (RIGHT - 1, OWN + WIDTH - 1))


def close_seams(ref, factors, which):
    for index in which:
        place, origin = SEAMS[index]
        value = ref[origin].astype(F32)
        turned = factors[2 * index].astype(F32) * value + factors[2 * index + 1].astype(F32) * pltpu.roll(value, 64, 1)
        ref[place] = turned.astype(BF)


def turn_factors(code):
    lane = lax.broadcasted_iota(jnp.int32, (16, 128), 1)
    side = jnp.where(lane < 64, -1.0, 1.0)
    keep = jnp.where(code == 0.0, 1.0, jnp.where(code == 2.0, -1.0, 0.0))
    swap = jnp.where(code == 1.0, side, jnp.where(code == 3.0, -side, 0.0))
    return keep.astype(BF), swap.astype(BF)


def state_kernel(fields_ref, after_ref, before_ref, own_ref, sibling_ref, far_ref, state_ref, weight_ref, semaphores):
    comp = lax.axis_index("comp")
    core = lax.rem(comp, 2)
    copies = [
        pltpu.make_async_copy(ref.at[0], weight_ref.at[place], semaphores.at[index])
        for index, (ref, place) in enumerate(
            ((own_ref, comp), (sibling_ref, comp + 1 - 2 * core), (far_ref, lax.rem(comp + 2, 4)))
        )
    ]
    for copy in copies:
        copy.start()

    def broadcast(tile, column):
        return jnp.broadcast_to(tile[:, column : column + 1], (16, 128))

    own_tile = fields_ref[2 * WIDTH].astype(F32)
    before_tile = before_ref[2 * DEPTH].astype(F32)
    after_tile = after_ref[2 * DEPTH].astype(F32)
    hidden, ocean, sea, factors = (
        state_ref.at[pl.ds(TOTAL * index, TOTAL if index < 3 else 2 * len(SEAMS))] for index in range(4)
    )
    for index, (tile, lane) in enumerate(((before_tile, 65), (own_tile, 64), (own_tile, 65), (after_tile, 64))):
        factors[2 * index], factors[2 * index + 1] = turn_factors(broadcast(tile, lane))
    for column in range(DEPTH):
        sea[column] = broadcast(before_tile, WIDTH - DEPTH + column).astype(BF)
        sea[RIGHT + column] = broadcast(after_tile, column).astype(BF)
    for column in range(WIDTH):
        sea[OWN + column] = broadcast(own_tile, column).astype(BF)
    nothing = jnp.zeros((2, 16, 128), BF)
    for ref in (ocean, sea):
        ref[pl.ds(DEPTH, 2)] = nothing
        ref[pl.ds(RIGHT - 2, 2)] = nothing
    for ref, origin, count, place in (
        (before_ref, 0, DEPTH, 0),
        (fields_ref, 0, WIDTH, OWN),
        (after_ref, 0, DEPTH, RIGHT),
    ):
        span = pl.ds(place, count)
        ocean_value = ref[pl.ds(origin + count, count)]
        ocean[span] = ocean_value
        atmos_value = ref[pl.ds(origin, count)].astype(F32)
        hidden[span] = (atmos_value + sea[span].astype(F32) * ocean_value.astype(F32)).astype(BF)
    close_seams(hidden, factors, range(4))
    for copy in copies:
        copy.wait()


def main_kernel(
    state_ref, weight_in, last_ref, atmos_out, ocean_out, weight_ref, hidden_ref, inner, ocean_ref, flux, final, semaphore
):
    comp = lax.axis_index("comp")
    last = 3 - comp
    copy = pltpu.make_async_copy(last_ref.at[0], weight_ref.at[last], semaphore)
    copy.start()

    def taps(section, which):
        return lambda index: weight_ref[section, which, index]

    hidden, ocean, sea, factors = (
        state_ref.at[pl.ds(TOTAL * index, TOTAL if index < 3 else 2 * len(SEAMS))] for index in range(4)
    )

    def load(ref, span):
        return ref[span].astype(F32)

    def convolve(source, weight, done, finish, out):
        bounds = (done, CUT - done, TOTAL - done)
        for part in range(2):
            start, stop = bounds[part : part + 2]
            span = pl.ds(start, stop - start)
            value = add_rows(product(source, weight, start, stop), stop - start)
            out[span] = finish(span, value).astype(BF)
            if done < DEPTH:
                close_seams(out, factors, (0, 1) if part == 0 else (2, 3))

    done = 0
    for step in range(STEPS):
        if step > 0:
            for start, stop, seams in ((done, CUT - done, (0, 1)), (CUT - done, TOTAL - done, (2, 3))):
                span = pl.ds(start, stop - start)
                hidden_ref[span] = (load(hidden, span) + load(sea, span) * load(ocean, span)).astype(BF)
                close_seams(hidden_ref, factors, seams)
        for section in range(4):
            source = hidden
            if section == 3:
                source = flux
                for start, stop, seams in ((done, CUT - done, (0, 1)), (CUT - done, TOTAL - done, (2, 3))):
                    span = pl.ds(start, stop - start)
                    flux[span] = (load(hidden, span) + load(ocean, span)).astype(BF)
                    close_seams(flux, factors, seams)
            if step == 0:
                pl.when(last == section)(copy.wait)
            done += 1
            convolve(source, taps(section, 0), done, lambda span, value: gelu(value), inner)
            done += 1
            if section == 3:
                base = ocean
                convolve(
                    inner, taps(section, 1), done,
                    lambda span, value: load(base, span) + load(sea, span) * value, ocean_ref,
                )
                ocean = ocean_ref
            else:
                base = hidden
                convolve(inner, taps(section, 1), done, lambda span, value: load(base, span) + value, hidden_ref)
                hidden = hidden_ref

    for source, out in ((hidden, atmos_out), (ocean, ocean_out)):
        final[...] = jnp.swapaxes(source[pl.ds(OWN, WIDTH)].astype(F32), 0, 1)
        for member in range(2):
            out[member] = final[pl.ds(member * 8 + 2 * comp, 2)].astype(BF)


def per_device(atmos_state, ocean_state, conv_weight, rotation, sea_mask):
    tiles = lax.axis_size("pix")
    vmem = pl.BlockSpec(memory_space=pltpu.VMEM)
    fields, down, up = pl.pallas_call(
        pack_kernel,
        out_shape=(
            pltpu.VMEM((2 * WIDTH + 1, 16, 128), BF),
            jax.ShapeDtypeStruct((2 * DEPTH + 1, 16, 128), BF),
            jax.ShapeDtypeStruct((2 * DEPTH + 1, 16, 128), BF),
        ),
        in_specs=[vmem, vmem, pl.BlockSpec(memory_space=pltpu.SMEM), vmem],
        out_specs=(vmem, vmem, vmem),
        scratch_shapes=[pltpu.VMEM((16, 128), F32)],
    )(atmos_state, ocean_state, rotation, sea_mask)

    names = ("pix", "comp")
    flip = 4 if tiles % 8 == 0 else 0
    swap = [(p * 4 + c, p * 4 + (c ^ 1)) for p in range(tiles) for c in range(4)]
    across = [(p * 4 + c, (p ^ flip) * 4 + (c ^ 2)) for p in range(tiles) for c in range(4)]
    far = lax.ppermute(conv_weight, names, across)
    rightward = [(i, (i + 1) % tiles) for i in range(tiles)]
    sibling = lax.ppermute(conv_weight, names, swap)
    after = lax.ppermute(down, "pix", [(j, i) for i, j in rightward])
    before = lax.ppermute(up, "pix", rightward)
    far, _ = lax.optimization_barrier((far, (up, down)))
    far_sibling = lax.ppermute(far, names, swap)

    anywhere = pl.BlockSpec(memory_space=pl.ANY)
    section_weights = pltpu.VMEM((4,) + conv_weight.shape[1:], BF)
    params = pltpu.CompilerParams(vmem_limit_bytes=40 << 20)
    state, weight = pl.pallas_call(
        state_kernel,
        out_shape=(pltpu.VMEM((3 * TOTAL + 2 * len(SEAMS), 16, 128), BF), section_weights),
        in_specs=[vmem, vmem, vmem, pl.BlockSpec(memory_space=pltpu.HBM), anywhere, anywhere],
        out_specs=(vmem, vmem),
        scratch_shapes=[pltpu.SemaphoreType.DMA((3,))],
        cost_estimate=pl.CostEstimate(flops=2 * 10**10, bytes_accessed=1 << 20, transcendentals=0),
        compiler_params=params,
    )(fields, after, before, pltpu.with_memory_space_constraint(conv_weight, pltpu.HBM), sibling, far)

    band = jax.ShapeDtypeStruct((2, 2, WIDTH, 128), BF)
    field = pltpu.VMEM((TOTAL, 16, 128), BF)
    return pl.pallas_call(
        main_kernel,
        out_shape=(band, band, section_weights),
        in_specs=[vmem, vmem, anywhere],
        out_specs=(vmem, vmem, vmem),
        input_output_aliases={1: 2},
        scratch_shapes=[field, field, field, field, pltpu.VMEM((16, WIDTH, 128), F32), pltpu.SemaphoreType.DMA(())],
        compiler_params=params,
    )(state, weight, far_sibling)[:2]


def solution(mesh):
    in_specs = (
        P(None, None, "pix", None),
        P(None, None, "pix", None),
        P("comp", None, None, None, None),
        P("pix", None),
        P(None, "pix"),
    )
    out_specs = (P(None, "comp", "pix", None), P(None, "comp", "pix", None))
    return jax.shard_map(
        per_device, mesh=mesh, in_specs=in_specs, out_specs=out_specs, check_vma=False
    )
```

```python
import functools

import jax
import jax.numpy as jnp
from jax import lax
from jax.experimental import pallas as pl
from jax.experimental.pallas import tpu as pltpu
from jax.sharding import PartitionSpec as P

STEPS = 2
BF = jnp.bfloat16
F32 = jnp.float32

DEPTH = 16
WIDTH = 32
OWN = DEPTH + 2
RIGHT = OWN + WIDTH + 2
TOTAL = RIGHT + DEPTH
PARTS = 4


def pack_kernel(atmos_ref, ocean_ref, rotation_ref, mask_ref, fields_ref, up_ref, down_ref, tile):
    for index, ref in enumerate((atmos_ref, ocean_ref)):
        value = ref[...].astype(F32).reshape(16, WIDTH, 128)
        value = jnp.swapaxes(value, 0, 1).astype(BF)
        fields_ref[pl.ds(index * WIDTH, WIDTH)] = value
        up_ref[pl.ds(index * DEPTH, DEPTH)] = value[WIDTH - DEPTH :]
        down_ref[pl.ds(index * DEPTH, DEPTH)] = value[:DEPTH]
    lane = lax.broadcasted_iota(jnp.int32, (16, 128), 1)
    first = rotation_ref[0, 0].astype(F32)
    second = rotation_ref[0, 1].astype(F32)
    tile[...] = jnp.where(lane == 64, first, jnp.where(lane == 65, second, 0.0))
    mask = mask_ref[...].astype(F32)
    tile[0:8, 0:WIDTH] = mask
    tile[8:16, 0:WIDTH] = mask
    packed = tile[...].astype(BF)
    fields_ref[2 * WIDTH] = packed
    up_ref[2 * DEPTH] = packed
    down_ref[2 * DEPTH] = packed


def shift_rows(value, by):
    count = value.shape[0]
    row = lax.broadcasted_iota(jnp.int32, (1, 8, 128), 1)
    rolled = pltpu.roll(value.reshape(count * 2, 8, 128), by % 8, 1)
    return jnp.where(row == (0 if by == 1 else 7), 0.0, rolled).reshape(count, 16, 128)


def convolve_columns(field, weight, start, stop):
    count = stop - start
    left = jnp.concatenate([ref[pl.ds(start + b - 1, count)] for b in range(3) for ref in field], axis=-1)
    nothing = jnp.zeros((128, 128), BF)
    right = []
    for b in range(3):
        right.append(jnp.concatenate([weight[3 + b], weight[6 + b]], axis=1))
        right.append(jnp.concatenate([weight[b], nothing], axis=1))
    value = lax.dot_general(
        left.reshape(count * 16, 768), jnp.concatenate(right, axis=0), (((1,), (0,)), ((), ())),
        preferred_element_type=F32,
    )
    return value[:, :128].reshape(count, 16, 128) + shift_rows(value[:, 128:].reshape(count, 16, 128), -1)


def store(field, span, value):
    field[0][span] = value.astype(BF)
    field[1][span] = shift_rows(value, 1).astype(BF)


def gelu(value):
    half = 0.5 * value
    return half + half * jnp.tanh(value * (0.7978845608028654 + 0.035677408136300125 * (value * value)))


SEAMS = ((DEPTH, OWN), (DEPTH + 1, DEPTH - 1), (OWN + WIDTH, RIGHT), (RIGHT - 1, OWN + WIDTH - 1))


def close_seams(field, factors):
    for ref in field:
        for index, (place, origin) in enumerate(SEAMS):
            value = ref[origin].astype(F32)
            keep, swap = factors[2 * index].astype(F32), factors[2 * index + 1].astype(F32)
            ref[place] = (keep * value + swap * pltpu.roll(value, 64, 1)).astype(BF)


def parts_of(state_ref):
    return [state_ref.at[pl.ds(TOTAL * index, TOTAL if index < 4 else 2 * len(SEAMS))] for index in range(5)]


def turn_factors(code):
    lane = lax.broadcasted_iota(jnp.int32, (16, 128), 1)
    side = jnp.where(lane < 64, -1.0, 1.0)
    keep = jnp.where(code == 0.0, 1.0, jnp.where(code == 2.0, -1.0, 0.0))
    swap = jnp.where(code == 1.0, side, jnp.where(code == 3.0, -side, 0.0))
    return keep.astype(BF), swap.astype(BF)


def state_kernel(fields_ref, before_ref, after_ref, own_ref, sibling_ref, far_ref, state_ref, weight_ref, semaphores):
    comp = lax.axis_index("comp")
    core = lax.rem(comp, 2)
    copies = [
        pltpu.make_async_copy(ref.at[0], weight_ref.at[place], semaphores.at[index])
        for index, (ref, place) in enumerate(
            ((own_ref, comp), (sibling_ref, comp + 1 - 2 * core), (far_ref, lax.rem(comp + 2, 4)))
        )
    ]
    for copy in copies:
        copy.start()

    def broadcast(tile, column):
        return jnp.broadcast_to(tile[:, column : column + 1], (16, 128))

    own_tile = fields_ref[2 * WIDTH].astype(F32)
    before_tile = before_ref[2 * DEPTH].astype(F32)
    after_tile = after_ref[2 * DEPTH].astype(F32)
    hidden, hidden_down, ocean, sea, factors = parts_of(state_ref)
    for index, (tile, lane) in enumerate(((before_tile, 65), (own_tile, 64), (own_tile, 65), (after_tile, 64))):
        factors[2 * index], factors[2 * index + 1] = turn_factors(broadcast(tile, lane))
    for column in range(DEPTH):
        sea[column] = broadcast(before_tile, WIDTH - DEPTH + column).astype(BF)
        sea[RIGHT + column] = broadcast(after_tile, column).astype(BF)
    for column in range(WIDTH):
        sea[OWN + column] = broadcast(own_tile, column).astype(BF)
    nothing = jnp.zeros((2, 16, 128), BF)
    for ref in (ocean, sea):
        ref[pl.ds(DEPTH, 2)] = nothing
        ref[pl.ds(RIGHT - 2, 2)] = nothing
    for ref, origin, count, place in (
        (before_ref, 0, DEPTH, 0),
        (fields_ref, 0, WIDTH, OWN),
        (after_ref, 0, DEPTH, RIGHT),
    ):
        span = pl.ds(place, count)
        ocean_value = ref[pl.ds(origin + count, count)]
        ocean[span] = ocean_value
        atmos_value = ref[pl.ds(origin, count)].astype(F32)
        store((hidden, hidden_down), span, atmos_value + sea[span].astype(F32) * ocean_value.astype(F32))
    close_seams((hidden, hidden_down), factors)
    for copy in copies:
        copy.wait()


def main_kernel(
    state_ref, weight_in, last_ref, atmos_out, ocean_out, weight_ref,
    hidden_ref, hidden_down, inner, inner_down, flux, flux_down, ocean_ref, final, semaphore,
):
    comp = lax.axis_index("comp")
    copy = pltpu.make_async_copy(last_ref.at[0], weight_ref.at[3 - comp], semaphore)
    copy.start()
    hidden, first_down, ocean, sea, factors = parts_of(state_ref)
    field = (hidden, first_down)
    copy.wait()

    def load(ref, span):
        return ref[span].astype(F32)

    def pieces(done):
        count = TOTAL - 2 * done
        bounds = [done + count * part // PARTS for part in range(PARTS + 1)]
        return zip(bounds[:-1], bounds[1:])

    done = 0
    for step in range(STEPS):
        if step > 0:
            for start, stop in pieces(done):
                span = pl.ds(start, stop - start)
                store(field, span, load(hidden, span) + load(sea, span) * load(ocean, span))
            close_seams(field, factors)
        for section in range(4):
            source = field
            if section == 3:
                source = (flux, flux_down)
                for start, stop in pieces(done):
                    span = pl.ds(start, stop - start)
                    store(source, span, load(hidden, span) + load(ocean, span))
                close_seams(source, factors)
            done += 1
            for start, stop in pieces(done):
                value = convolve_columns(source, weight_ref.at[section, 0], start, stop)
                store((inner, inner_down), pl.ds(start, stop - start), gelu(value))
            close_seams((inner, inner_down), factors)
            done += 1
            for start, stop in pieces(done):
                span = pl.ds(start, stop - start)
                value = convolve_columns((inner, inner_down), weight_ref.at[section, 1], start, stop)
                if section == 3:
                    ocean_ref[span] = (load(ocean, span) + load(sea, span) * value).astype(BF)
                else:
                    store((hidden_ref, hidden_down), span, load(hidden, span) + value)
            if section == 3:
                ocean = ocean_ref
            else:
                hidden, field = hidden_ref, (hidden_ref, hidden_down)
                close_seams(field, factors)

    for source, out in ((hidden, atmos_out), (ocean, ocean_out)):
        final[...] = jnp.swapaxes(source[pl.ds(OWN, WIDTH)].astype(F32), 0, 1)
        for member in range(2):
            out[member] = final[pl.ds(member * 8 + 2 * comp, 2)].astype(BF)


def per_device(atmos_state, ocean_state, conv_weight, rotation, sea_mask):
    tiles = lax.axis_size("pix")
    vmem = pl.BlockSpec(memory_space=pltpu.VMEM)
    fields, up, down = pl.pallas_call(
        pack_kernel,
        out_shape=(
            pltpu.VMEM((2 * WIDTH + 1, 16, 128), BF),
            jax.ShapeDtypeStruct((2 * DEPTH + 1, 16, 128), BF),
            jax.ShapeDtypeStruct((2 * DEPTH + 1, 16, 128), BF),
        ),
        in_specs=[vmem, vmem, pl.BlockSpec(memory_space=pltpu.SMEM), vmem],
        out_specs=(vmem, vmem, vmem),
        scratch_shapes=[pltpu.VMEM((16, 128), F32)],
    )(atmos_state, ocean_state, rotation, sea_mask)

    names = ("pix", "comp")
    flip = 4 if tiles % 8 == 0 else 0
    swap = [(p * 4 + c, p * 4 + (c ^ 1)) for p in range(tiles) for c in range(4)]
    across = [(p * 4 + c, (p ^ flip) * 4 + (c ^ 2)) for p in range(tiles) for c in range(4)]
    far = lax.ppermute(conv_weight, names, across)
    rightward = [(i, (i + 1) % tiles) for i in range(tiles)]
    sibling = lax.ppermute(conv_weight, names, swap)
    before = lax.ppermute(up, "pix", rightward)
    after = lax.ppermute(down, "pix", [(j, i) for i, j in rightward])
    far, _ = lax.optimization_barrier((far, (up, down)))
    far_sibling = lax.ppermute(far, names, swap)

    anywhere = pl.BlockSpec(memory_space=pl.ANY)
    section_weights = pltpu.VMEM((4,) + conv_weight.shape[1:], BF)
    params = pltpu.CompilerParams(vmem_limit_bytes=40 << 20)
    state, weight = pl.pallas_call(
        state_kernel,
        out_shape=(pltpu.VMEM((4 * TOTAL + 2 * len(SEAMS), 16, 128), BF), section_weights),
        in_specs=[vmem, vmem, vmem, pl.BlockSpec(memory_space=pltpu.HBM), anywhere, anywhere],
        out_specs=(vmem, vmem),
        scratch_shapes=[pltpu.SemaphoreType.DMA((3,))],
        cost_estimate=pl.CostEstimate(flops=2 * 10**10, bytes_accessed=1 << 20, transcendentals=0),
        compiler_params=params,
    )(fields, before, after, pltpu.with_memory_space_constraint(conv_weight, pltpu.HBM), sibling, far)

    band = jax.ShapeDtypeStruct((2, 2, WIDTH, 128), BF)
    field = pltpu.VMEM((TOTAL, 16, 128), BF)
    return pl.pallas_call(
        main_kernel,
        out_shape=(band, band, section_weights),
        in_specs=[vmem, vmem, anywhere],
        out_specs=(vmem, vmem, vmem),
        input_output_aliases={1: 2},
        scratch_shapes=[field] * 7 + [pltpu.VMEM((16, WIDTH, 128), F32), pltpu.SemaphoreType.DMA(())],
        compiler_params=params,
    )(state, weight, far_sibling)[:2]


def solution(mesh):
    in_specs = (
        P(None, None, "pix", None),
        P(None, None, "pix", None),
        P("comp", None, None, None, None),
        P("pix", None),
        P(None, "pix"),
    )
    out_specs = (P(None, "comp", "pix", None), P(None, "comp", "pix", None))
    return jax.shard_map(
        per_device, mesh=mesh, in_specs=in_specs, out_specs=out_specs, check_vma=False
    )
```

```python
import functools

import jax
import jax.numpy as jnp
from jax import lax
from jax.experimental import pallas as pl
from jax.experimental.pallas import tpu as pltpu
from jax.sharding import PartitionSpec as P

STEPS = 2
BF = jnp.bfloat16
F32 = jnp.float32

DEPTH = 16
WIDTH = 32
OWN = DEPTH + 2
RIGHT = OWN + WIDTH + 2
TOTAL = RIGHT + DEPTH
PARTS = 6


def pack_kernel(
    atmos_ref, ocean_ref, rotation_ref, mask_ref, own_ref, fields_ref, up_ref, down_ref, own_out, tile, semaphore
):
    copy = pltpu.make_async_copy(own_ref.at[0], own_out, semaphore)
    copy.start()
    for index, ref in enumerate((atmos_ref, ocean_ref)):
        value = ref[...].astype(F32).reshape(16, WIDTH, 128)
        value = jnp.swapaxes(value, 0, 1).astype(BF)
        fields_ref[pl.ds(index * WIDTH, WIDTH)] = value
        up_ref[pl.ds(index * DEPTH, DEPTH)] = value[WIDTH - DEPTH :]
        down_ref[pl.ds(index * DEPTH, DEPTH)] = value[:DEPTH]
    lane = lax.broadcasted_iota(jnp.int32, (16, 128), 1)
    first = rotation_ref[0, 0].astype(F32)
    second = rotation_ref[0, 1].astype(F32)
    tile[...] = jnp.where(lane == 64, first, jnp.where(lane == 65, second, 0.0))
    mask = mask_ref[...].astype(F32)
    tile[0:8, 0:WIDTH] = mask
    tile[8:16, 0:WIDTH] = mask
    packed = tile[...].astype(BF)
    fields_ref[2 * WIDTH] = packed
    up_ref[2 * DEPTH] = packed
    down_ref[2 * DEPTH] = packed
    copy.wait()


def shift_rows(value, by):
    count = value.shape[0]
    row = lax.broadcasted_iota(jnp.int32, (1, 8, 128), 1)
    rolled = pltpu.roll(value.reshape(count * 2, 8, 128), by % 8, 1)
    return jnp.where(row == (0 if by == 1 else 7), 0.0, rolled).reshape(count, 16, 128)


def convolve_columns(field, weight, start, stop):
    count = stop - start
    left = jnp.concatenate([ref[pl.ds(start + b - 1, count)] for b in range(3) for ref in field], axis=-1)
    nothing = jnp.zeros((128, 128), BF)
    right = []
    for b in range(3):
        right.append(jnp.concatenate([weight[3 + b], weight[6 + b]], axis=1))
        right.append(jnp.concatenate([weight[b], nothing], axis=1))
    value = lax.dot_general(
        left.reshape(count * 16, 768), jnp.concatenate(right, axis=0), (((1,), (0,)), ((), ())),
        preferred_element_type=F32,
    )
    return value[:, :128].reshape(count, 16, 128) + shift_rows(value[:, 128:].reshape(count, 16, 128), -1)


def store(field, span, value):
    field[0][span] = value.astype(BF)
    field[1][span] = shift_rows(value, 1).astype(BF)


def gelu(value):
    half = 0.5 * value
    return half + half * jnp.tanh(value * (0.7978845608028654 + 0.035677408136300125 * (value * value)))


SEAMS = ((DEPTH, OWN), (DEPTH + 1, DEPTH - 1), (OWN + WIDTH, RIGHT), (RIGHT - 1, OWN + WIDTH - 1))


def close_seams(field, factors):
    for ref in field:
        for index, (place, origin) in enumerate(SEAMS):
            value = ref[origin].astype(F32)
            keep, swap = factors[2 * index].astype(F32), factors[2 * index + 1].astype(F32)
            ref[place] = (keep * value + swap * pltpu.roll(value, 64, 1)).astype(BF)


def parts_of(state_ref):
    return [state_ref.at[pl.ds(TOTAL * index, TOTAL if index < 4 else 2 * len(SEAMS))] for index in range(5)]


def turn_factors(code):
    lane = lax.broadcasted_iota(jnp.int32, (16, 128), 1)
    side = jnp.where(lane < 64, -1.0, 1.0)
    keep = jnp.where(code == 0.0, 1.0, jnp.where(code == 2.0, -1.0, 0.0))
    swap = jnp.where(code == 1.0, side, jnp.where(code == 3.0, -side, 0.0))
    return keep.astype(BF), swap.astype(BF)


def state_kernel(fields_ref, before_ref, after_ref, own_ref, sibling_ref, far_ref, state_ref, weight_ref):
    comp = lax.axis_index("comp")
    weight_ref[comp] = own_ref[...]
    weight_ref[comp + 1 - 2 * lax.rem(comp, 2)] = sibling_ref[0]
    weight_ref[lax.rem(comp + 2, 4)] = far_ref[0]

    def broadcast(tile, column):
        return jnp.broadcast_to(tile[:, column : column + 1], (16, 128))

    own_tile = fields_ref[2 * WIDTH].astype(F32)
    before_tile = before_ref[2 * DEPTH].astype(F32)
    after_tile = after_ref[2 * DEPTH].astype(F32)
    hidden, hidden_down, ocean, sea, factors = parts_of(state_ref)
    for index, (tile, lane) in enumerate(((before_tile, 65), (own_tile, 64), (own_tile, 65), (after_tile, 64))):
        factors[2 * index], factors[2 * index + 1] = turn_factors(broadcast(tile, lane))
    for column in range(DEPTH):
        sea[column] = broadcast(before_tile, WIDTH - DEPTH + column).astype(BF)
        sea[RIGHT + column] = broadcast(after_tile, column).astype(BF)
    for column in range(WIDTH):
        sea[OWN + column] = broadcast(own_tile, column).astype(BF)
    nothing = jnp.zeros((2, 16, 128), BF)
    for ref in (ocean, sea):
        ref[pl.ds(DEPTH, 2)] = nothing
        ref[pl.ds(RIGHT - 2, 2)] = nothing
    for ref, origin, count, place in (
        (before_ref, 0, DEPTH, 0),
        (fields_ref, 0, WIDTH, OWN),
        (after_ref, 0, DEPTH, RIGHT),
    ):
        span = pl.ds(place, count)
        ocean_value = ref[pl.ds(origin + count, count)]
        ocean[span] = ocean_value
        atmos_value = ref[pl.ds(origin, count)].astype(F32)
        store((hidden, hidden_down), span, atmos_value + sea[span].astype(F32) * ocean_value.astype(F32))
    close_seams((hidden, hidden_down), factors)


def main_kernel(
    state_ref, weight_in, last_ref, atmos_out, ocean_out, weight_ref,
    hidden_ref, hidden_down, inner, inner_down, flux, flux_down, ocean_ref, final,
):
    comp = lax.axis_index("comp")
    weight_ref[3 - comp] = last_ref[0]
    hidden, first_down, ocean, sea, factors = parts_of(state_ref)
    field = (hidden, first_down)

    def load(ref, span):
        return ref[span].astype(F32)

    def pieces(done):
        count = TOTAL - 2 * done
        bounds = [done + count * part // PARTS for part in range(PARTS + 1)]
        return zip(bounds[:-1], bounds[1:])

    done = 0
    for step in range(STEPS):
        if step > 0:
            for start, stop in pieces(done):
                span = pl.ds(start, stop - start)
                store(field, span, load(hidden, span) + load(sea, span) * load(ocean, span))
            close_seams(field, factors)
        for section in range(4):
            source = field
            if section == 3:
                source = (flux, flux_down)
                for start, stop in pieces(done):
                    span = pl.ds(start, stop - start)
                    store(source, span, load(hidden, span) + load(ocean, span))
                close_seams(source, factors)
            done += 1
            for start, stop in pieces(done):
                value = convolve_columns(source, weight_ref.at[section, 0], start, stop)
                store((inner, inner_down), pl.ds(start, stop - start), gelu(value))
            close_seams((inner, inner_down), factors)
            done += 1
            for start, stop in pieces(done):
                span = pl.ds(start, stop - start)
                value = convolve_columns((inner, inner_down), weight_ref.at[section, 1], start, stop)
                if section == 3:
                    ocean_ref[span] = (load(ocean, span) + load(sea, span) * value).astype(BF)
                else:
                    store((hidden_ref, hidden_down), span, load(hidden, span) + value)
            if section == 3:
                ocean = ocean_ref
            else:
                hidden, field = hidden_ref, (hidden_ref, hidden_down)
                close_seams(field, factors)

    for source, out in ((hidden, atmos_out), (ocean, ocean_out)):
        final[...] = jnp.swapaxes(source[pl.ds(OWN, WIDTH)].astype(F32), 0, 1)
        for member in range(2):
            out[member] = final[pl.ds(member * 8 + 2 * comp, 2)].astype(BF)


def per_device(atmos_state, ocean_state, conv_weight, rotation, sea_mask):
    tiles = lax.axis_size("pix")
    vmem = pl.BlockSpec(memory_space=pltpu.VMEM)
    fields, up, down, own = pl.pallas_call(
        pack_kernel,
        out_shape=(
            pltpu.VMEM((2 * WIDTH + 1, 16, 128), BF),
            jax.ShapeDtypeStruct((2 * DEPTH + 1, 16, 128), BF),
            jax.ShapeDtypeStruct((2 * DEPTH + 1, 16, 128), BF),
            pltpu.VMEM(conv_weight.shape[1:], BF),
        ),
        in_specs=[vmem, vmem, pl.BlockSpec(memory_space=pltpu.SMEM), vmem, pl.BlockSpec(memory_space=pltpu.HBM)],
        out_specs=(vmem, vmem, vmem, vmem),
        scratch_shapes=[pltpu.VMEM((16, 128), F32), pltpu.SemaphoreType.DMA(())],
    )(atmos_state, ocean_state, rotation, sea_mask, pltpu.with_memory_space_constraint(conv_weight, pltpu.HBM))

    names = ("pix", "comp")
    flip = 4 if tiles % 8 == 0 else 0
    swap = [(p * 4 + c, p * 4 + (c ^ 1)) for p in range(tiles) for c in range(4)]
    across = [(p * 4 + c, (p ^ flip) * 4 + (c ^ 2)) for p in range(tiles) for c in range(4)]
    far = lax.ppermute(conv_weight, names, across)
    rightward = [(i, (i + 1) % tiles) for i in range(tiles)]
    sibling = lax.ppermute(conv_weight, names, swap)
    before = lax.ppermute(up, "pix", rightward)
    after = lax.ppermute(down, "pix", [(j, i) for i, j in rightward])
    far, _ = lax.optimization_barrier((far, (up, down)))
    far_sibling = lax.ppermute(far, names, swap)

    section_weights = pltpu.VMEM((4,) + conv_weight.shape[1:], BF)
    params = pltpu.CompilerParams(vmem_limit_bytes=40 << 20)
    state, weight = pl.pallas_call(
        state_kernel,
        out_shape=(pltpu.VMEM((4 * TOTAL + 2 * len(SEAMS), 16, 128), BF), section_weights),
        in_specs=[vmem] * 6,
        out_specs=(vmem, vmem),
        cost_estimate=pl.CostEstimate(flops=2 * 10**10, bytes_accessed=1 << 20, transcendentals=0),
        compiler_params=params,
    )(fields, before, after, own, sibling, far)

    band = jax.ShapeDtypeStruct((2, 2, WIDTH, 128), BF)
    field = pltpu.VMEM((TOTAL, 16, 128), BF)
    return pl.pallas_call(
        main_kernel,
        out_shape=(band, band, section_weights),
        in_specs=[vmem, vmem, vmem],
        out_specs=(vmem, vmem, vmem),
        input_output_aliases={1: 2},
        scratch_shapes=[field] * 7 + [pltpu.VMEM((16, WIDTH, 128), F32)],
        compiler_params=params,
    )(state, weight, far_sibling)[:2]


def solution(mesh):
    in_specs = (
        P(None, None, "pix", None),
        P(None, None, "pix", None),
        P("comp", None, None, None, None),
        P("pix", None),
        P(None, "pix"),
    )
    out_specs = (P(None, "comp", "pix", None), P(None, "comp", "pix", None))
    return jax.shard_map(
        per_device, mesh=mesh, in_specs=in_specs, out_specs=out_specs, check_vma=False
    )
```

```python
import functools

import jax
import jax.numpy as jnp
from jax import lax
from jax.experimental import pallas as pl
from jax.experimental.pallas import tpu as pltpu
from jax.sharding import PartitionSpec as P

STEPS = 2
BF = jnp.bfloat16
F32 = jnp.float32

DEPTH = 16
WIDTH = 32
OWN = DEPTH + 2
RIGHT = OWN + WIDTH + 2
TOTAL = RIGHT + DEPTH
PARTS = 6


def pack_kernel(atmos_ref, ocean_ref, rotation_ref, mask_ref, fields_ref, up_ref, down_ref, tile):
    for index, ref in enumerate((atmos_ref, ocean_ref)):
        value = ref[...].astype(F32).reshape(16, WIDTH, 128)
        value = jnp.swapaxes(value, 0, 1).astype(BF)
        fields_ref[pl.ds(index * WIDTH, WIDTH)] = value
        up_ref[pl.ds(index * DEPTH, DEPTH)] = value[WIDTH - DEPTH :]
        down_ref[pl.ds(index * DEPTH, DEPTH)] = value[:DEPTH]
    lane = lax.broadcasted_iota(jnp.int32, (16, 128), 1)
    first = rotation_ref[0, 0].astype(F32)
    second = rotation_ref[0, 1].astype(F32)
    tile[...] = jnp.where(lane == 64, first, jnp.where(lane == 65, second, 0.0))
    mask = mask_ref[...].astype(F32)
    tile[0:8, 0:WIDTH] = mask
    tile[8:16, 0:WIDTH] = mask
    packed = tile[...].astype(BF)
    fields_ref[2 * WIDTH] = packed
    up_ref[2 * DEPTH] = packed
    down_ref[2 * DEPTH] = packed


def shift_rows(value, by):
    count = value.shape[0]
    row = lax.broadcasted_iota(jnp.int32, (1, 8, 128), 1)
    rolled = pltpu.roll(value.reshape(count * 2, 8, 128), by % 8, 1)
    return jnp.where(row == (0 if by == 1 else 7), 0.0, rolled).reshape(count, 16, 128)


def convolve_columns(field, weight, start, stop):
    count = stop - start
    left = jnp.concatenate([ref[pl.ds(start + b - 1, count)] for b in range(3) for ref in field], axis=-1)
    nothing = jnp.zeros((128, 128), BF)
    right = []
    for b in range(3):
        right.append(jnp.concatenate([weight[3 + b], weight[6 + b]], axis=1))
        right.append(jnp.concatenate([weight[b], nothing], axis=1))
    value = lax.dot_general(
        left.reshape(count * 16, 768), jnp.concatenate(right, axis=0), (((1,), (0,)), ((), ())),
        preferred_element_type=F32,
    )
    return value[:, :128].reshape(count, 16, 128) + shift_rows(value[:, 128:].reshape(count, 16, 128), -1)


def store(field, span, value):
    field[0][span] = value.astype(BF)
    field[1][span] = shift_rows(value, 1).astype(BF)


def gelu(value):
    half = 0.5 * value
    return half + half * jnp.tanh(value * (0.7978845608028654 + 0.035677408136300125 * (value * value)))


SEAMS = ((DEPTH, OWN), (DEPTH + 1, DEPTH - 1), (OWN + WIDTH, RIGHT), (RIGHT - 1, OWN + WIDTH - 1))


def close_seams(field, factors):
    for ref in field:
        for index, (place, origin) in enumerate(SEAMS):
            value = ref[origin].astype(F32)
            keep, swap = factors[2 * index].astype(F32), factors[2 * index + 1].astype(F32)
            ref[place] = (keep * value + swap * pltpu.roll(value, 64, 1)).astype(BF)


def parts_of(state_ref):
    return [state_ref.at[pl.ds(TOTAL * index, TOTAL if index < 4 else 2 * len(SEAMS))] for index in range(5)]


def turn_factors(code):
    lane = lax.broadcasted_iota(jnp.int32, (16, 128), 1)
    side = jnp.where(lane < 64, -1.0, 1.0)
    keep = jnp.where(code == 0.0, 1.0, jnp.where(code == 2.0, -1.0, 0.0))
    swap = jnp.where(code == 1.0, side, jnp.where(code == 3.0, -side, 0.0))
    return keep.astype(BF), swap.astype(BF)


def state_kernel(fields_ref, before_ref, after_ref, sibling_ref, far_ref, state_ref, weight_ref):
    comp = lax.axis_index("comp")
    weight_ref[comp + 1 - 2 * lax.rem(comp, 2)] = sibling_ref[0]
    weight_ref[lax.rem(comp + 2, 4)] = far_ref[0]

    def broadcast(tile, column):
        return jnp.broadcast_to(tile[:, column : column + 1], (16, 128))

    own_tile = fields_ref[2 * WIDTH].astype(F32)
    before_tile = before_ref[2 * DEPTH].astype(F32)
    after_tile = after_ref[2 * DEPTH].astype(F32)
    hidden, hidden_down, ocean, sea, factors = parts_of(state_ref)
    for index, (tile, lane) in enumerate(((before_tile, 65), (own_tile, 64), (own_tile, 65), (after_tile, 64))):
        factors[2 * index], factors[2 * index + 1] = turn_factors(broadcast(tile, lane))
    for column in range(DEPTH):
        sea[column] = broadcast(before_tile, WIDTH - DEPTH + column).astype(BF)
        sea[RIGHT + column] = broadcast(after_tile, column).astype(BF)
    for column in range(WIDTH):
        sea[OWN + column] = broadcast(own_tile, column).astype(BF)
    nothing = jnp.zeros((2, 16, 128), BF)
    for ref in (ocean, sea):
        ref[pl.ds(DEPTH, 2)] = nothing
        ref[pl.ds(RIGHT - 2, 2)] = nothing
    for ref, origin, count, place in (
        (before_ref, 0, DEPTH, 0),
        (fields_ref, 0, WIDTH, OWN),
        (after_ref, 0, DEPTH, RIGHT),
    ):
        span = pl.ds(place, count)
        ocean_value = ref[pl.ds(origin + count, count)]
        ocean[span] = ocean_value
        atmos_value = ref[pl.ds(origin, count)].astype(F32)
        store((hidden, hidden_down), span, atmos_value + sea[span].astype(F32) * ocean_value.astype(F32))
    close_seams((hidden, hidden_down), factors)


def main_kernel(
    state_ref, weight_in, last_ref, own_ref, atmos_out, ocean_out, weight_ref,
    hidden_ref, hidden_down, inner, inner_down, flux, flux_down, ocean_ref, final, semaphore,
):
    comp = lax.axis_index("comp")
    copy = pltpu.make_async_copy(own_ref.at[0], weight_ref.at[comp], semaphore)
    copy.start()
    weight_ref[3 - comp] = last_ref[0]
    hidden, first_down, ocean, sea, factors = parts_of(state_ref)
    field = (hidden, first_down)

    def load(ref, span):
        return ref[span].astype(F32)

    def pieces(done):
        count = TOTAL - 2 * done
        bounds = [done + count * part // PARTS for part in range(PARTS + 1)]
        return zip(bounds[:-1], bounds[1:])

    done = 0
    for step in range(STEPS):
        if step > 0:
            for start, stop in pieces(done):
                span = pl.ds(start, stop - start)
                store(field, span, load(hidden, span) + load(sea, span) * load(ocean, span))
            close_seams(field, factors)
        for section in range(4):
            source = field
            if section == 3:
                source = (flux, flux_down)
                for start, stop in pieces(done):
                    span = pl.ds(start, stop - start)
                    store(source, span, load(hidden, span) + load(ocean, span))
                close_seams(source, factors)
            if step == 0 and section < 2:
                pl.when(comp == 0 if section == 0 else comp != 0)(copy.wait)
            done += 1
            for start, stop in pieces(done):
                value = convolve_columns(source, weight_ref.at[section, 0], start, stop)
                store((inner, inner_down), pl.ds(start, stop - start), gelu(value))
            close_seams((inner, inner_down), factors)
            done += 1
            for start, stop in pieces(done):
                span = pl.ds(start, stop - start)
                value = convolve_columns((inner, inner_down), weight_ref.at[section, 1], start, stop)
                if section == 3:
                    ocean_ref[span] = (load(ocean, span) + load(sea, span) * value).astype(BF)
                else:
                    store((hidden_ref, hidden_down), span, load(hidden, span) + value)
            if section == 3:
                ocean = ocean_ref
            else:
                hidden, field = hidden_ref, (hidden_ref, hidden_down)
                close_seams(field, factors)

    for source, out in ((hidden, atmos_out), (ocean, ocean_out)):
        final[...] = jnp.swapaxes(source[pl.ds(OWN, WIDTH)].astype(F32), 0, 1)
        for member in range(2):
            out[member] = final[pl.ds(member * 8 + 2 * comp, 2)].astype(BF)


def per_device(atmos_state, ocean_state, conv_weight, rotation, sea_mask):
    tiles = lax.axis_size("pix")
    vmem = pl.BlockSpec(memory_space=pltpu.VMEM)
    fields, up, down = pl.pallas_call(
        pack_kernel,
        out_shape=(
            pltpu.VMEM((2 * WIDTH + 1, 16, 128), BF),
            jax.ShapeDtypeStruct((2 * DEPTH + 1, 16, 128), BF),
            jax.ShapeDtypeStruct((2 * DEPTH + 1, 16, 128), BF),
        ),
        in_specs=[vmem, vmem, pl.BlockSpec(memory_space=pltpu.SMEM), vmem],
        out_specs=(vmem, vmem, vmem),
        scratch_shapes=[pltpu.VMEM((16, 128), F32)],
    )(atmos_state, ocean_state, rotation, sea_mask)

    names = ("pix", "comp")
    flip = 4 if tiles % 8 == 0 else 0
    swap = [(p * 4 + c, p * 4 + (c ^ 1)) for p in range(tiles) for c in range(4)]
    across = [(p * 4 + c, (p ^ flip) * 4 + (c ^ 2)) for p in range(tiles) for c in range(4)]
    far = lax.ppermute(conv_weight, names, across)
    rightward = [(i, (i + 1) % tiles) for i in range(tiles)]
    sibling = lax.ppermute(conv_weight, names, swap)
    before = lax.ppermute(up, "pix", rightward)
    after = lax.ppermute(down, "pix", [(j, i) for i, j in rightward])
    far, _ = lax.optimization_barrier((far, (up, down)))
    far_sibling = lax.ppermute(far, names, swap)

    section_weights = pltpu.VMEM((4,) + conv_weight.shape[1:], BF)
    params = pltpu.CompilerParams(vmem_limit_bytes=40 << 20)
    state, weight = pl.pallas_call(
        state_kernel,
        out_shape=(pltpu.VMEM((4 * TOTAL + 2 * len(SEAMS), 16, 128), BF), section_weights),
        in_specs=[vmem] * 5,
        out_specs=(vmem, vmem),
        cost_estimate=pl.CostEstimate(flops=2 * 10**10, bytes_accessed=1 << 20, transcendentals=0),
        compiler_params=params,
    )(fields, before, after, sibling, far)

    band = jax.ShapeDtypeStruct((2, 2, WIDTH, 128), BF)
    field = pltpu.VMEM((TOTAL, 16, 128), BF)
    return pl.pallas_call(
        main_kernel,
        out_shape=(band, band, section_weights),
        in_specs=[vmem, vmem, vmem, pl.BlockSpec(memory_space=pltpu.HBM)],
        out_specs=(vmem, vmem, vmem),
        input_output_aliases={1: 2},
        scratch_shapes=[field] * 7 + [pltpu.VMEM((16, WIDTH, 128), F32), pltpu.SemaphoreType.DMA(())],
        compiler_params=params,
    )(state, weight, far_sibling, pltpu.with_memory_space_constraint(conv_weight, pltpu.HBM))[:2]


def solution(mesh):
    in_specs = (
        P(None, None, "pix", None),
        P(None, None, "pix", None),
        P("comp", None, None, None, None),
        P("pix", None),
        P(None, "pix"),
    )
    out_specs = (P(None, "comp", "pix", None), P(None, "comp", "pix", None))
    return jax.shard_map(
        per_device, mesh=mesh, in_specs=in_specs, out_specs=out_specs, check_vma=False
    )
```

```python
import functools

import jax
import jax.numpy as jnp
from jax import lax
from jax.experimental import pallas as pl
from jax.experimental.pallas import tpu as pltpu
from jax.sharding import PartitionSpec as P

STEPS = 2
BF = jnp.bfloat16
F32 = jnp.float32

DEPTH = 16
WIDTH = 32
OWN = DEPTH + 2
RIGHT = OWN + WIDTH + 2
TOTAL = RIGHT + DEPTH
PARTS = 8


def pack_kernel(atmos_ref, ocean_ref, rotation_ref, mask_ref, fields_ref, up_ref, down_ref, tile):
    for index, ref in enumerate((atmos_ref, ocean_ref)):
        value = ref[...].astype(F32).reshape(16, WIDTH, 128)
        value = jnp.swapaxes(value, 0, 1).astype(BF)
        fields_ref[pl.ds(index * WIDTH, WIDTH)] = value
        up_ref[pl.ds(index * DEPTH, DEPTH)] = value[WIDTH - DEPTH :]
        down_ref[pl.ds(index * DEPTH, DEPTH)] = value[:DEPTH]
    lane = lax.broadcasted_iota(jnp.int32, (16, 128), 1)
    first = rotation_ref[0, 0].astype(F32)
    second = rotation_ref[0, 1].astype(F32)
    tile[...] = jnp.where(lane == 64, first, jnp.where(lane == 65, second, 0.0))
    mask = mask_ref[...].astype(F32)
    tile[0:8, 0:WIDTH] = mask
    tile[8:16, 0:WIDTH] = mask
    packed = tile[...].astype(BF)
    fields_ref[2 * WIDTH] = packed
    up_ref[2 * DEPTH] = packed
    down_ref[2 * DEPTH] = packed


def shift_rows(value, by):
    count = value.shape[0]
    row = lax.broadcasted_iota(jnp.int32, (1, 8, 128), 1)
    rolled = pltpu.roll(value.reshape(count * 2, 8, 128), by % 8, 1)
    return jnp.where(row == (0 if by == 1 else 7), 0.0, rolled).reshape(count, 16, 128)


def convolve_columns(field, weight, start, stop):
    count = stop - start
    left = jnp.concatenate([ref[pl.ds(start + b - 1, count)] for b in range(3) for ref in field], axis=-1)
    nothing = jnp.zeros((128, 128), BF)
    right = []
    for b in range(3):
        right.append(jnp.concatenate([weight[3 + b], weight[6 + b]], axis=1))
        right.append(jnp.concatenate([weight[b], nothing], axis=1))
    value = lax.dot_general(
        left.reshape(count * 16, 768), jnp.concatenate(right, axis=0), (((1,), (0,)), ((), ())),
        preferred_element_type=F32,
    )
    return value[:, :128].reshape(count, 16, 128) + shift_rows(value[:, 128:].reshape(count, 16, 128), -1)


def store(field, span, value):
    field[0][span] = value.astype(BF)
    field[1][span] = shift_rows(value, 1).astype(BF)


def gelu(value):
    half = 0.5 * value
    return half + half * jnp.tanh(value * (0.7978845608028654 + 0.035677408136300125 * (value * value)))


SEAMS = ((DEPTH, OWN), (DEPTH + 1, DEPTH - 1), (OWN + WIDTH, RIGHT), (RIGHT - 1, OWN + WIDTH - 1))


def close_seams(field, factors):
    for ref in field:
        for index, (place, origin) in enumerate(SEAMS):
            value = ref[origin].astype(F32)
            keep, swap = factors[2 * index].astype(F32), factors[2 * index + 1].astype(F32)
            ref[place] = (keep * value + swap * pltpu.roll(value, 64, 1)).astype(BF)


def parts_of(state_ref):
    return [state_ref.at[pl.ds(TOTAL * index, TOTAL if index < 4 else 2 * len(SEAMS))] for index in range(5)]


def turn_factors(code):
    lane = lax.broadcasted_iota(jnp.int32, (16, 128), 1)
    side = jnp.where(lane < 64, -1.0, 1.0)
    keep = jnp.where(code == 0.0, 1.0, jnp.where(code == 2.0, -1.0, 0.0))
    swap = jnp.where(code == 1.0, side, jnp.where(code == 3.0, -side, 0.0))
    return keep.astype(BF), swap.astype(BF)


def state_kernel(fields_ref, before_ref, after_ref, sibling_ref, far_ref, state_ref, weight_ref):
    comp = lax.axis_index("comp")
    weight_ref[comp + 1 - 2 * lax.rem(comp, 2)] = sibling_ref[0]
    weight_ref[lax.rem(comp + 2, 4)] = far_ref[0]

    def broadcast(tile, column):
        return jnp.broadcast_to(tile[:, column : column + 1], (16, 128))

    own_tile = fields_ref[2 * WIDTH].astype(F32)
    before_tile = before_ref[2 * DEPTH].astype(F32)
    after_tile = after_ref[2 * DEPTH].astype(F32)
    hidden, hidden_down, ocean, sea, factors = parts_of(state_ref)
    for index, (tile, lane) in enumerate(((before_tile, 65), (own_tile, 64), (own_tile, 65), (after_tile, 64))):
        factors[2 * index], factors[2 * index + 1] = turn_factors(broadcast(tile, lane))
    for column in range(DEPTH):
        sea[column] = broadcast(before_tile, WIDTH - DEPTH + column).astype(BF)
        sea[RIGHT + column] = broadcast(after_tile, column).astype(BF)
    for column in range(WIDTH):
        sea[OWN + column] = broadcast(own_tile, column).astype(BF)
    nothing = jnp.zeros((2, 16, 128), BF)
    for ref in (ocean, sea):
        ref[pl.ds(DEPTH, 2)] = nothing
        ref[pl.ds(RIGHT - 2, 2)] = nothing
    for ref, origin, count, place in (
        (before_ref, 0, DEPTH, 0),
        (fields_ref, 0, WIDTH, OWN),
        (after_ref, 0, DEPTH, RIGHT),
    ):
        span = pl.ds(place, count)
        ocean_value = ref[pl.ds(origin + count, count)]
        ocean[span] = ocean_value
        atmos_value = ref[pl.ds(origin, count)].astype(F32)
        store((hidden, hidden_down), span, atmos_value + sea[span].astype(F32) * ocean_value.astype(F32))
    close_seams((hidden, hidden_down), factors)


def main_kernel(
    state_ref, weight_in, last_ref, own_ref, atmos_out, ocean_out, weight_ref,
    hidden_ref, hidden_down, inner, inner_down, flux, flux_down, ocean_ref, final, semaphore,
):
    comp = lax.axis_index("comp")
    copy = pltpu.make_async_copy(own_ref.at[0], weight_ref.at[comp], semaphore)
    copy.start()
    weight_ref[3 - comp] = last_ref[0]
    hidden, first_down, ocean, sea, factors = parts_of(state_ref)
    field = (hidden, first_down)

    def load(ref, span):
        return ref[span].astype(F32)

    def pieces(done):
        count = TOTAL - 2 * done
        bounds = [done + count * part // PARTS for part in range(PARTS + 1)]
        return zip(bounds[:-1], bounds[1:])

    done = 0
    for step in range(STEPS):
        if step > 0:
            for start, stop in pieces(done):
                span = pl.ds(start, stop - start)
                store(field, span, load(hidden, span) + load(sea, span) * load(ocean, span))
            close_seams(field, factors)
        for section in range(4):
            source = field
            if section == 3:
                source = (flux, flux_down)
                for start, stop in pieces(done):
                    span = pl.ds(start, stop - start)
                    store(source, span, load(hidden, span) + load(ocean, span))
                close_seams(source, factors)
            if step == 0 and section < 2:
                pl.when(comp == 0 if section == 0 else comp != 0)(copy.wait)
            done += 1
            for start, stop in pieces(done):
                value = convolve_columns(source, weight_ref.at[section, 0], start, stop)
                store((inner, inner_down), pl.ds(start, stop - start), gelu(value))
            close_seams((inner, inner_down), factors)
            done += 1
            for start, stop in pieces(done):
                span = pl.ds(start, stop - start)
                value = convolve_columns((inner, inner_down), weight_ref.at[section, 1], start, stop)
                if section == 3:
                    ocean_ref[span] = (load(ocean, span) + load(sea, span) * value).astype(BF)
                else:
                    store((hidden_ref, hidden_down), span, load(hidden, span) + value)
            if section == 3:
                ocean = ocean_ref
            else:
                hidden, field = hidden_ref, (hidden_ref, hidden_down)
                close_seams(field, factors)

    for source, out in ((hidden, atmos_out), (ocean, ocean_out)):
        final[...] = jnp.swapaxes(source[pl.ds(OWN, WIDTH)].astype(F32), 0, 1)
        for member in range(2):
            out[member] = final[pl.ds(member * 8 + 2 * comp, 2)].astype(BF)


def per_device(atmos_state, ocean_state, conv_weight, rotation, sea_mask):
    tiles = lax.axis_size("pix")
    vmem = pl.BlockSpec(memory_space=pltpu.VMEM)
    fields, up, down = pl.pallas_call(
        pack_kernel,
        out_shape=(
            pltpu.VMEM((2 * WIDTH + 1, 16, 128), BF),
            jax.ShapeDtypeStruct((2 * DEPTH + 1, 16, 128), BF),
            jax.ShapeDtypeStruct((2 * DEPTH + 1, 16, 128), BF),
        ),
        in_specs=[vmem, vmem, pl.BlockSpec(memory_space=pltpu.SMEM), vmem],
        out_specs=(vmem, vmem, vmem),
        scratch_shapes=[pltpu.VMEM((16, 128), F32)],
    )(atmos_state, ocean_state, rotation, sea_mask)

    names = ("pix", "comp")
    flip = 4 if tiles % 8 == 0 else 0
    swap = [(p * 4 + c, p * 4 + (c ^ 1)) for p in range(tiles) for c in range(4)]
    across = [(p * 4 + c, (p ^ flip) * 4 + (c ^ 2)) for p in range(tiles) for c in range(4)]
    far = lax.ppermute(conv_weight, names, across)
    rightward = [(i, (i + 1) % tiles) for i in range(tiles)]
    sibling = lax.ppermute(conv_weight, names, swap)
    before = lax.ppermute(up, "pix", rightward)
    after = lax.ppermute(down, "pix", [(j, i) for i, j in rightward])
    far, _ = lax.optimization_barrier((far, (up, down)))
    far_sibling = lax.ppermute(far, names, swap)

    section_weights = pltpu.VMEM((4,) + conv_weight.shape[1:], BF)
    params = pltpu.CompilerParams(vmem_limit_bytes=40 << 20)
    state, weight = pl.pallas_call(
        state_kernel,
        out_shape=(pltpu.VMEM((4 * TOTAL + 2 * len(SEAMS), 16, 128), BF), section_weights),
        in_specs=[vmem] * 5,
        out_specs=(vmem, vmem),
        cost_estimate=pl.CostEstimate(flops=2 * 10**10, bytes_accessed=1 << 20, transcendentals=0),
        compiler_params=params,
    )(fields, before, after, sibling, far)

    band = jax.ShapeDtypeStruct((2, 2, WIDTH, 128), BF)
    field = pltpu.VMEM((TOTAL, 16, 128), BF)
    return pl.pallas_call(
        main_kernel,
        out_shape=(band, band, section_weights),
        in_specs=[vmem, vmem, vmem, pl.BlockSpec(memory_space=pltpu.HBM)],
        out_specs=(vmem, vmem, vmem),
        input_output_aliases={1: 2},
        scratch_shapes=[field] * 7 + [pltpu.VMEM((16, WIDTH, 128), F32), pltpu.SemaphoreType.DMA(())],
        compiler_params=params,
    )(state, weight, far_sibling, pltpu.with_memory_space_constraint(conv_weight, pltpu.HBM))[:2]


def solution(mesh):
    in_specs = (
        P(None, None, "pix", None),
        P(None, None, "pix", None),
        P("comp", None, None, None, None),
        P("pix", None),
        P(None, "pix"),
    )
    out_specs = (P(None, "comp", "pix", None), P(None, "comp", "pix", None))
    return jax.shard_map(
        per_device, mesh=mesh, in_specs=in_specs, out_specs=out_specs, check_vma=False
    )
```
